512 devices in a mesh: group: 16 (over z), sub: 32 (over x, y, core).
Axes of the slice: x: 4, y: 4, z: 16, core: 2. Of those that a mesh axis runs over, the one named last changes fastest.
Arguments:
- schur_blocks: bfloat16 [16, 32, 32, 14, 4096], P('group', 'sub'), may hold values from -0.1875 to 0.1875
- block_cols: int32 [16, 32, 32, 14], P('group', 'sub'), may hold values from 0 to 31
- basis: bfloat16 [16, 32, 32, 1024], P('group', 'sub'), may hold values from -6 to 6
- owners: int32 [16, 32, 32, 1], P('group', 'sub'), may hold values from 0 to 31; in each aligned block of 32 rows (0 to 31, 32 to 63, ..., all dimensions but the last counted through in order) at most 4 rows name the same one
- targets: int32 [16, 32, 32], P('group', 'sub'), may hold values from 0 to 31
- inverses: float32 [16, 32, 32, 4096], P('group', 'sub'), may hold values from -0.75 to 0.75
- coarse_map: int32 [16, 32, 16], P('group', 'sub'), may hold values from 0 to 511
Outputs:
- corrected: float32 [16, 32, 32, 1024], P('group', 'sub')
- coarse_matrix: float32 [512, 512], P('sub')
The draws below stay inside these ranges and needn't reach their ends.
Inputs may be any that keep to these rules, and one draw needn't show every extreme that they name: `owners`: among the 32 blocks of one subdomain at most 4 name the same owner.
All inputs are finite; a program needn't handle non-finite values.
Results may differ from the reference program's by a relative error of at most 0.0066.
Values may be sent and summed in bfloat16 or wider, within the bound.
A program may use at most 64 MiB of HBM per device.

```python
import math
import jax
import jax.numpy as jnp
import numpy as np
from jax import lax

BS = 64
NB = 32
KB = 14
NC = 16
CAP = 4
OWN = 32
COARSE = 512
N_GROUP = 16
N_SUB = 32


def plant(entries, stream_key, least, top_value):
    longest = entries.shape.index(max(entries.shape))
    spots = []
    for shift in (0, 1):
        where = [jax.random.randint(jax.random.fold_in(stream_key, axis), (), 0, length) for axis, length in enumerate(entries.shape)]
        where[longest] = (where[longest] + shift) % entries.shape[longest]
        spots.append(tuple(where))
    return entries.at[spots[0]].set(least).at[spots[1]].set(top_value)


def block_levels(stream_key, dims, pieces, least, top_value):
    def one(axis_at, shards_of):
        heights = jax.random.uniform(jax.random.fold_in(jax.random.fold_in(stream_key, 6), axis_at), (shards_of,), jnp.float32, least / len(pieces), top_value / len(pieces))
        return jnp.repeat(jnp.exp(heights), dims[axis_at] // shards_of).reshape((-1,) + (1,) * (len(dims) - axis_at - 1))

    level = one(*pieces[0])
    for cut in pieces[1:]:
        level = level * one(*cut)
    return level


def routed_block(own_key, own, number, rows, number_of, top, bound, lean):
    order = jax.random.permutation(own_key, number_of)
    crowded, usual = portions_of(number_of, rows * top, bound, lean, True), portions_of(number_of, rows * top, bound, lean, False)
    places = jnp.arange(number_of)

    def named(tallies, rotation):
        used = int((tallies > 0).sum())
        fixed = max(1, used // 4)
        passed = fixed + (places - fixed + rotation * (used - fixed)) % max(1, number_of - fixed)
        return jnp.zeros((number_of,), jnp.int32).at[order[jnp.where(places < fixed, places, passed)]].set(jnp.asarray(tallies, jnp.int32))

    tallies = jnp.where(number % 4 == 0, named(crowded, number // 4), named(usual, number - number // 4 - 1))
    mixed = jax.random.permutation(jax.random.fold_in(own, 3), number_of)
    source_of, receiver = mixed[0:number_of // 2 * 2:2], mixed[1:number_of // 2 * 2:2]
    room = jnp.minimum(tallies[source_of] - 1, bound - tallies[receiver]) // 2
    room = jnp.where((source_of == order[0]) | (receiver == order[0]) | (tallies[receiver] == 0), 0, jnp.maximum(room, 0))
    passed = jax.random.randint(jax.random.fold_in(own, 4), (number_of // 2,), 0, 1 << 20) % (room + 1)
    tallies = tallies.at[source_of].add(-passed).at[receiver].add(passed)
    items = jnp.searchsorted(jnp.cumsum(tallies), jnp.arange(rows * top), side="right").astype(jnp.int32)
    table = items.reshape(top, rows).T
    table = table[jax.random.permutation(jax.random.fold_in(own, 1), rows)]
    rotation = jax.random.randint(jax.random.fold_in(own, 2), (rows, 1), 0, top)
    return jnp.take_along_axis(table, (jnp.arange(top)[None, :] + rotation) % top, axis=1)


def portions_of(count, total, reach, slope, full):
    loads = [(1 << 20) // math.isqrt(standing ** slope) + 1 for standing in range(1, count + 1)]
    largest = reach if full else min(reach, max(-(-total // count), total * loads[0] // sum(loads)))
    least = 1 if total - largest >= count - 1 else 0
    holding, rest = [largest] + [least] * (count - 1), total - largest - least * (count - 1)
    while rest > 0:
        free = [i for i in range(1, count) if holding[i] < largest] or [i for i in range(1, count) if holding[i] < reach]
        pool, budget = sum([loads[i] for i in free]), rest
        for i in free:
            addition = min(reach - holding[i], max(1, budget * loads[i] // pool), rest)
            holding[i] = holding[i] + addition
            rest = rest - addition
    return np.array(holding)


def scatter_about(own_key, extent, deviation, reach, shards=(), kind=jnp.bfloat16):
    array = jax.random.normal(own_key, extent, jnp.float32) * deviation
    if len(shards) > 0:
        array = block_levels(own_key, extent, shards, -0.22, 0.18) * array
    return jnp.clip(array, min=-reach, max=reach).astype(kind)


def setup_inputs(seed: int = 0) -> dict:
    splits = jax.random.split(jax.random.key(seed), 8)
    schur_blocks = scatter_about(splits[0], (N_GROUP, N_SUB, NB, KB, BS * BS), (KB * BS) ** -0.5, 0.1875, ((0, 16), (1, 32)))
    block_cols = plant(jax.random.randint(splits[1], (N_GROUP, N_SUB, NB, KB), 0, NB), jax.random.fold_in(splits[1], 1), 0, NB - 1).astype(jnp.int32)
    basis = scatter_about(splits[2], (N_GROUP, N_SUB, NB, NC * BS), 1.0, 6.0, ((0, 16), (1, 32)))
    owners_keys = jax.random.split(jax.random.fold_in(splits[3], 1), N_GROUP * N_SUB * NB // NB)
    owners_turns = jax.random.permutation(jax.random.fold_in(splits[3], 3), N_GROUP * N_SUB * NB // NB)
    owners = jax.vmap(lambda own, number: routed_block(jax.random.fold_in(splits[3], 2), own, number, NB, N_SUB, 1, CAP, 2))(owners_keys, owners_turns).reshape((N_GROUP, N_SUB, NB, 1))
    targets = plant(jax.random.randint(splits[4], (N_GROUP, N_SUB, NB), 0, OWN), jax.random.fold_in(splits[4], 1), 0, OWN - 1).astype(jnp.int32)
    inverses = scatter_about(splits[5], (N_GROUP, N_SUB, OWN, BS * BS), BS ** -0.5, 0.75, ((0, 16), (1, 32)), jnp.float32)
    coarse_map = plant(jax.random.randint(splits[6], (N_GROUP, N_SUB, NC), 0, COARSE), jax.random.fold_in(splits[6], 1), 0, COARSE - 1).astype(jnp.int32)
    return dict(schur_blocks=schur_blocks, block_cols=block_cols, basis=basis, owners=owners, targets=targets, inverses=inverses, coarse_map=coarse_map)


def block_product(blocks, cols, vectors):
    nb = blocks.shape[0]
    kb = blocks.shape[1]
    mats = blocks.reshape(nb, kb, BS, BS).astype(jnp.float32)
    picked = vectors[cols].reshape(nb, kb, NC, BS).astype(jnp.float32)
    out = jnp.einsum('bkij,bkcj->bci', mats, picked, precision=lax.Precision.HIGHEST)
    return out.reshape(nb, NC * BS)


def group_product(args):
    return jax.vmap(block_product)(*args)


def reference(schur_blocks, block_cols, basis, owners, targets, inverses, coarse_map):
    partial_value = lax.map(group_product, (schur_blocks, block_cols, basis)).astype(jnp.bfloat16)
    flat = (owners[..., 0] * NB + targets).reshape(N_GROUP, N_SUB * NB).astype(jnp.int32)
    def assemble(values, index):
        return jax.ops.segment_sum(values.reshape(N_SUB * NB, NC * BS).astype(jnp.float32), index, num_segments=N_SUB * OWN)
    assembled = jax.vmap(assemble)(partial_value, flat).reshape(N_GROUP, N_SUB, OWN, NC, BS)
    mats = inverses.reshape(N_GROUP, N_SUB, OWN, BS, BS)
    corrected = jnp.einsum('gsjci,gsjik->gsjck', assembled, mats, precision=lax.Precision.HIGHEST).reshape(N_GROUP, N_SUB, OWN, NC * BS)
    rounded = corrected.astype(jnp.bfloat16)
    def pick(values, index):
        return values.reshape(N_SUB * OWN, NC * BS)[index]
    returned = jax.vmap(pick)(rounded, flat).reshape(N_GROUP, N_SUB, NB, NC * BS)
    adjusted = (basis.astype(jnp.float32) - returned.astype(jnp.float32)).astype(jnp.bfloat16)
    image = lax.map(group_product, (schur_blocks, block_cols, adjusted))
    local = jnp.einsum('gsbci,gsbei->gsce', adjusted.astype(jnp.float32).reshape(N_GROUP, N_SUB, NB, NC, BS), image.reshape(N_GROUP, N_SUB, NB, NC, BS), precision=lax.Precision.HIGHEST)
    local = local * (NB * BS) ** -0.5
    rows_index = jnp.broadcast_to(coarse_map[..., :, None], local.shape)
    cols_index = jnp.broadcast_to(coarse_map[..., None, :], local.shape)
    coarse_matrix = jnp.zeros((COARSE, COARSE), jnp.float32).at[rows_index, cols_index].add(local)
    return corrected, coarse_matrix
```

```python
import functools

import jax
import jax.numpy as jnp
from jax import lax
from jax.experimental import pallas as pl
from jax.experimental.pallas import tpu as pltpu
from jax.sharding import PartitionSpec as P

MESH = pl.DeviceIdType.MESH
F32 = jnp.float32
BF16 = jnp.bfloat16
NB = 32
KB = 14
S = 32
G = 16
CAP = 4
COARSE = 512
CHUNKS = 7


def iota(shape, axis):
    return lax.broadcasted_iota(jnp.int32, shape, axis)


def hot(condition):
    return jnp.where(condition, 1.0, 0.0).astype(BF16)


def dot(a, b):
    return jnp.dot(a, b, preferred_element_type=F32)


def dot_t(a, b):
    return lax.dot_general(a, b, (((1,), (1,)), ((), ())), preferred_element_type=F32)


def lanes(v):
    return pl.ds(128 * v, 128)


def sub_peer(s, step):
    x = lax.rem(lax.div(s, 8) + lax.div(step, 8), 4)
    y = lax.rem(lax.div(s, 2) + lax.div(step, 2), 4)
    core = lax.rem(s + step, 2)
    return x * 8 + y * 2 + core


def group_peer(g, step):
    return lax.rem(g + step, G)


def spread(x):
    x3 = x.reshape(NB, 8, 128)
    r3 = pltpu.roll(x, 64, 1).reshape(NB, 8, 128)
    low = iota((NB, 8, 128), 2) < 64
    parts = [jnp.where(low, x3, 0.0), jnp.where(low, r3, 0.0), jnp.where(low, 0.0, r3), jnp.where(low, 0.0, x3)]
    return jnp.concatenate(parts, axis=1).astype(BF16)


def kernel(
    schur, cols, basis, owner, target, inverse, cmap,
    corrected, matrix,
    raw, packed, vecs, natural, rows_f32, select_t, table, send, arrive, right, pair, back, returned,
    left_g, high_g, low_g, terms, piece, pieces, final, load_sem, sem,
):
    g, s = lax.axis_index("group"), lax.axis_index("sub")

    def each(count, function):
        def body(step, carry):
            function(step)
            return carry

        lax.fori_loop(1, count, body, 0)

    def to_sub(source_of, into, k):
        def one(step):
            d = sub_peer(s, step)
            pltpu.make_async_remote_copy(
                src_ref=source_of(d), dst_ref=into.at[s], send_sem=sem.at[2 * k], recv_sem=sem.at[2 * k + 1],
                device_id={"sub": d}, device_id_type=MESH,
            ).start()

        each(S, one)

    def to_group(source_of, into, k):
        def one(step):
            d = group_peer(g, step)
            pltpu.make_async_remote_copy(
                src_ref=source_of(d), dst_ref=into.at[g], send_sem=sem.at[2 * k], recv_sem=sem.at[2 * k + 1],
                device_id={"group": d}, device_id_type=MESH,
            ).start()

        each(G, one)

    def settle(buffer, count, which):
        part = buffer.at[pl.ds(0, count)]
        pltpu.make_async_copy(part, part, sem.at[which]).wait()

    barrier = pltpu.get_barrier_semaphore()
    each(S, lambda step: pl.semaphore_signal(barrier, 1, device_id={"sub": sub_peer(s, step)}, device_id_type=MESH))
    each(G, lambda step: pl.semaphore_signal(barrier, 1, device_id={"group": group_peer(g, step)}, device_id_type=MESH))

    per = KB // CHUNKS

    def load(c):
        part = pl.ds(per * c, per)
        return pltpu.make_async_copy(schur.at[part], raw.at[part], load_sem.at[c])

    for c in range(CHUNKS):
        load(c).start()

    lane32 = iota((NB, 128), 1)
    row32 = iota((NB, 128), 0)
    eye32 = iota((NB, NB), 0) == iota((NB, NB), 1)
    own = jnp.sum(jnp.where(eye32, owner[...], 0), axis=1, keepdims=True) == lane32 // CAP
    below = hot(iota((NB, NB), 1) < iota((NB, NB), 0))
    seen = dot(below, hot(own)).astype(jnp.int32)
    taken = own & (seen == lane32 % CAP)
    target_col = jnp.sum(jnp.where(eye32, target[...].astype(F32), 0.0), axis=1, keepdims=True)
    slot_target = jnp.sum(jnp.where(taken, target_col + 1.0, 0.0), axis=0, keepdims=True)
    slot_col = jnp.sum(jnp.where(taken, lane32.astype(F32), 0.0), axis=1, keepdims=True)
    slot_row = jnp.sum(jnp.where(eye32, slot_col, 0.0), axis=0, keepdims=True)
    eye16 = iota((16, 16), 0) == iota((16, 16), 1)
    cmap_col = jnp.sum(jnp.where(eye16, cmap[...], 0), axis=1, keepdims=True)
    lane16 = iota((16, 128), 1)
    ordered = (lane16 < 16) & (iota((16, 128), 0) == 2 * (lane16 % 8) + lane16 // 8)
    map_high = jnp.sum(jnp.where(ordered, (cmap_col // 16).astype(F32), 0.0), axis=0, keepdims=True)
    map_low = jnp.sum(jnp.where(ordered, (cmap_col % 16).astype(F32), 0.0), axis=0, keepdims=True)
    table[s] = jnp.concatenate([slot_target, map_high, map_low, jnp.zeros((5, 128), F32)], axis=0)

    flat = jnp.concatenate([basis[:, lanes(u)] for u in range(8)], axis=0)
    r256, c256 = iota((256, 256), 0), iota((256, 256), 1)
    by_block = hot((c256 % NB == r256 // 8) & (c256 // NB == r256 % 8))
    nat = dot(by_block, flat)
    natural[...] = nat
    vecs[...] = spread(nat)

    regroup = hot((c256 % 16 == r256 // 16) & (c256 // 16 == r256 % 16))

    def unpack(k, half):
        at = pl.ds(pl.multiple_of(16 * half, 16), 16)
        sides = []
        for h in range(2):
            sides.append(jnp.concatenate([raw[k, at, lanes(16 * h + t)] for t in range(16)], axis=0))
        out = dot(regroup, jnp.concatenate(sides, axis=1)).astype(BF16)
        for h in range(2):
            for b in range(16):
                packed[16 * half + b, pl.ds(16 * h, 16), lanes(k)] = out[16 * b : 16 * b + 16, 128 * h : 128 * h + 128]

    for c in range(CHUNKS):
        load(c).wait()
        for k in range(per * c, per * c + per):

            def some(half, carry, k=k):
                unpack(k, half)
                return carry

            lax.fori_loop(0, 2, some, 0)

    pl.semaphore_wait(barrier, S - 1 + G - 1)
    to_sub(lambda d: table.at[s], table, 0)

    def product(b):
        vectors = jnp.concatenate([vecs[cols[k, b]] for k in range(KB)], axis=1)
        block = packed[b]
        out = dot_t(vectors, jnp.concatenate([block] * 4, axis=0))
        return [out[8 * v : 8 * v + 8] for v in range(4)]

    group8 = iota((8, 128), 1) // 32

    def first(b, carry):
        r = product(b)
        value = jnp.where(group8 == 0, r[0], jnp.where(group8 == 1, r[1], jnp.where(group8 == 2, r[2], r[3])))
        rows_f32[pl.ds(pl.multiple_of(8 * b, 8), 8), :] = value
        return carry

    lax.fori_loop(0, NB, first, 0, unroll=4)

    widen = hot(iota((NB, 256), 1) // 8 == iota((NB, 256), 0))
    slot_lane = dot(jnp.broadcast_to(slot_row, (8, NB)).astype(BF16), widen)[0:1].astype(jnp.int32)
    code = slot_lane // CAP * 32 + iota((1, 256), 1) % 8 * CAP + slot_lane % CAP
    select = hot(iota((1024, 256), 0) == code)
    send[...] = dot(select, rows_f32[...].astype(BF16)).astype(BF16).reshape(S, 32, 128)
    to_sub(lambda d: send.at[d], arrive, 1)
    arrive[s] = send[s]

    tall = hot(iota((256, NB), 0) // 8 == iota((256, NB), 1))
    slot_tall = dot(tall, jnp.broadcast_to(slot_col, (NB, 128)).astype(BF16)).astype(jnp.int32)
    code_tall = slot_tall // CAP * 32 + iota((256, 128), 0) % 8 * CAP + slot_tall % CAP
    for v in range(8):
        select_t[:, lanes(v)] = hot(iota((256, 128), 1) + 128 * v == code_tall)

    for jg in range(4):
        tiles = jnp.stack([inverse[pl.ds(8 * jg, 8), lanes(t)] for t in range(32)], axis=0)
        block = jnp.swapaxes(tiles, 0, 1)
        turned = pltpu.roll(block.reshape(256, 128), 64, 1).reshape(8, 32, 128)
        low = iota((8, 32, 128), 2) < 64
        parts = [jnp.where(low, block, 0.0), jnp.where(low, 0.0, turned), jnp.where(low, turned, 0.0), jnp.where(low, 0.0, block)]
        right[pl.ds(8 * jg, 8)] = jnp.concatenate(parts, axis=1).astype(BF16)

    settle(table, S - 1, 1)
    mine = jnp.where(lane32 // CAP == s, table[:, 0, :], 0.0).astype(BF16)
    by_slot = hot(iota((128, 1024), 0) % CAP == iota((128, 1024), 1) % CAP)
    spread_slot = dot(mine, by_slot)
    named = jnp.sum(jnp.where(iota((NB, 1024), 0) == iota((NB, 1024), 1) // 32, spread_slot, 0.0), axis=0, keepdims=True)
    code_in = (named.astype(jnp.int32) - 1) * 8 + iota((1, 1024), 1) // CAP % 8
    gather = hot(iota((256, 1024), 0) == code_in)
    by_source = hot(iota((1024, NB), 0) // 32 == iota((1024, NB), 1))
    tall_slot = dot(by_source, mine)
    kept = jnp.where(iota((1024, 128), 0) % CAP == iota((1024, 128), 1) % CAP, tall_slot, 0.0).astype(BF16)
    named_t = dot(kept, jnp.full((128, 256), 1.0, BF16)).astype(jnp.int32)
    gather_t = hot(iota((1024, 256), 1) == (named_t - 1) * 8 + iota((1024, 256), 0) // CAP % 8)

    settle(arrive, S - 1, 3)
    assembled = dot(gather, arrive[...].reshape(1024, 128))
    high = assembled.astype(BF16).astype(F32)
    pair[...] = jnp.concatenate(
        [high.reshape(NB, 8, 128), (assembled - high).reshape(NB, 8, 128)], axis=1
    ).astype(BF16)

    def correct(j, carry):
        out = dot(pair[j], right[j])
        rows_f32[pl.ds(pl.multiple_of(8 * j, 8), 8), :] = out[0:8] + out[8:16]
        return carry

    lax.fori_loop(0, NB, correct, 0, unroll=8)
    back[...] = dot(gather_t, rows_f32[...].astype(BF16)).astype(BF16).reshape(S, 32, 128)
    to_sub(lambda d: back.at[d], returned, 2)
    returned[s] = back[s]
    for u in range(8):
        corrected[:, lanes(u)] = rows_f32[pl.ds(u, NB, stride=8), :]

    erep_l = iota((128, 256), 1)
    copies = hot(iota((128, 256), 0) == erep_l // 128 * 16 + erep_l % 16)
    maps_h = table[:, 1, :].astype(BF16)
    maps_l = table[:, 2, :].astype(BF16)
    ll = iota((128, 1024), 1)
    pick = hot(iota((128, 1024), 0) == ll // 64 % 2 * 8 + ll % 8)
    source = ll[0:NB] // 256 * 8 + ll[0:NB] // 8 % 8
    is_source = iota((NB, 1024), 0) == source
    lane_h = jnp.sum(jnp.where(is_source, dot(maps_h, pick), 0.0), axis=0, keepdims=True).astype(jnp.int32)
    lane_l = jnp.sum(jnp.where(is_source, dot(maps_l, pick), 0.0), axis=0, keepdims=True).astype(jnp.int32)
    rows_mine = hot((iota((16, 1024), 0) == lane_l) & (lane_h == s))
    tall_s = hot(iota((512, NB), 0) // 16 == iota((512, NB), 1))
    own_lane = iota((512, 128), 0) % 16 == iota((512, 128), 1)
    col_h = jnp.where(own_lane, dot(tall_s, maps_h), 0.0).astype(BF16)
    col_l = jnp.where(own_lane, dot(tall_s, maps_l), 0.0).astype(BF16)
    ones = jnp.full((128, COARSE), 1.0, BF16)
    place = (dot(col_h, ones) * 16.0 + dot(col_l, ones)).astype(jnp.int32)
    spread_cols = hot(place == iota((512, COARSE), 1))

    settle(returned, S - 1, 5)
    from_owner = dot(select_t[...], returned[...].reshape(1024, 128))
    adjusted = (natural[...] - from_owner).astype(BF16)
    vecs[...] = spread(adjusted.astype(F32))
    q_row, q_col = iota((128, 128), 0), iota((128, 128), 1)
    reorder = hot((q_row // 64 == q_col // 32 % 2) & (q_row % 2 == q_col // 64) & (q_row % 64 // 2 == q_col % 32))
    message = dot(adjusted, reorder).reshape(NB, 8, 128)
    for b in range(NB):
        left_g[:, lanes(b)] = jnp.concatenate([message[b], jnp.zeros((8, 128), F32)], axis=0).astype(BF16)

    def second(b, carry):
        r = product(b)
        at_low = group8 < 2
        p_low = group8 % 2 == 0
        one, two = jnp.where(at_low, r[0], r[2]), jnp.where(at_low, r[1], r[3])
        rows = jnp.concatenate(
            [jnp.where(p_low, one, 0.0), jnp.where(p_low, two, 0.0), jnp.where(p_low, 0.0, one), jnp.where(p_low, 0.0, two)],
            axis=0,
        )
        top = rows.astype(BF16)
        at = pl.ds(pl.multiple_of(128 * b, 128), 128)
        high_g[:, at] = top
        low_g[:, at] = (rows - top.astype(F32)).astype(BF16)
        return carry

    lax.fori_loop(0, NB, second, 0, unroll=4)
    galerkin = (dot_t(left_g[...], high_g[...]) + dot_t(left_g[...], low_g[...])) * (NB * 64) ** -0.5
    terms[s] = jnp.concatenate([galerkin[0:8], jnp.zeros((8, 96), F32)], axis=1)
    to_sub(lambda d: terms.at[s], terms, 3)

    settle(terms, S - 1, 7)
    every = terms[...].reshape(256, 128)
    top = every.astype(BF16)
    both = jnp.concatenate([top, (every - top.astype(F32)).astype(BF16)], axis=0)
    wide = dot(both, copies)
    wide_row, wide_lane = iota((512, 256), 0), iota((512, 256), 1)
    wide = jnp.where(wide_row // 8 % 8 == wide_lane // 16 % 8, wide, 0.0).astype(BF16)
    parts = []
    for v in range(4):
        pieces_v = [wide[256 * h + 64 * v : 256 * h + 64 * v + 64, 128 * p : 128 * p + 128] for h in range(2) for p in range(2)]
        parts.append(dot(rows_mine[:, 256 * v : 256 * v + 256], jnp.concatenate(pieces_v, axis=0)))
    part = jnp.concatenate(parts, axis=1)
    p1 = part.astype(BF16).astype(F32)
    p2 = (part - p1).astype(BF16).astype(F32)
    p3 = part - p1 - p2
    out = dot(jnp.concatenate([p1, p2, p3], axis=0).astype(BF16), spread_cols)
    out = out[0:16] + out[16:32] + out[32:48]
    for v in range(G):
        piece[v] = out[4 * (v // 4) : 4 * (v // 4) + 4, 128 * (v % 4) : 128 * (v % 4) + 128]
    to_group(lambda d: piece.at[d], pieces, 4)
    pieces[g] = piece[g]
    settle(pieces, G - 1, 9)
    total = pieces[0]
    for v in range(1, G):
        total = total + pieces[v]
    final[g] = total
    to_group(lambda d: final.at[g], final, 5)
    settle(final, G - 1, 11)
    for v in range(G):
        matrix[pl.ds(4 * (v // 4), 4), lanes(v % 4)] = final[v]

    settle(table, S - 1, 0)
    settle(send, S - 1, 2)
    settle(back, S - 1, 4)
    settle(terms, S - 1, 6)
    settle(piece, G - 1, 8)
    settle(final, G - 1, 10)


def on_device(schur_blocks, block_cols, basis, owners, targets, inverses, coarse_map):
    vmem = pl.BlockSpec(memory_space=pltpu.VMEM)
    corrected, matrix = pl.pallas_call(
        kernel,
        out_shape=(jax.ShapeDtypeStruct((NB, 1024), F32), jax.ShapeDtypeStruct((16, COARSE), F32)),
        in_specs=[pl.BlockSpec(memory_space=pltpu.HBM), pl.BlockSpec(memory_space=pltpu.SMEM)] + [vmem] * 5,
        out_specs=(vmem, vmem),
        scratch_shapes=[
            pltpu.VMEM((KB, NB, 4096), BF16),
            pltpu.VMEM((NB, 32, 128 * KB), BF16),
            pltpu.VMEM((NB, 32, 128), BF16),
            pltpu.VMEM((256, 128), F32),
            pltpu.VMEM((256, 128), F32),
            pltpu.VMEM((256, 1024), BF16),
            pltpu.VMEM((S, 8, 128), F32),
            pltpu.VMEM((S, 32, 128), BF16),
            pltpu.VMEM((S, 32, 128), BF16),
            pltpu.VMEM((NB, 128, 128), BF16),
            pltpu.VMEM((NB, 16, 128), BF16),
            pltpu.VMEM((S, 32, 128), BF16),
            pltpu.VMEM((S, 32, 128), BF16),
            pltpu.VMEM((16, 128 * NB), BF16),
            pltpu.VMEM((32, 128 * NB), BF16),
            pltpu.VMEM((32, 128 * NB), BF16),
            pltpu.VMEM((S, 8, 128), F32),
            pltpu.VMEM((G, 4, 128), F32),
            pltpu.VMEM((G, 4, 128), F32),
            pltpu.VMEM((G, 4, 128), F32),
            pltpu.SemaphoreType.DMA((CHUNKS,)),
            pltpu.SemaphoreType.DMA((12,)),
        ],
        compiler_params=pltpu.CompilerParams(
            collective_id=0, has_side_effects=True, vmem_limit_bytes=48 * 1024 * 1024
        ),
        name="setup_pass",
    )(
        jnp.swapaxes(schur_blocks[0, 0], 0, 1),
        block_cols[0, 0].T,
        basis[0, 0],
        owners[0, :, :, 0],
        targets[0],
        inverses[0, 0],
        coarse_map[0],
    )
    return corrected[None, None], matrix


def solution(mesh):
    return jax.shard_map(
        on_device,
        mesh=mesh,
        in_specs=(
            P("group", "sub", None, None, None),
            P("group", "sub", None, None),
            P("group", "sub", None, None),
            P("group", "sub", None, None),
            P("group", "sub", None),
            P("group", "sub", None, None),
            P("group", "sub", None),
        ),
        out_specs=(P("group", "sub", None, None), P("sub", None)),
        check_vma=False,
    )
```

```python
import functools

import jax
import jax.numpy as jnp
from jax import lax
from jax.experimental import pallas as pl
from jax.experimental.pallas import tpu as pltpu
from jax.sharding import PartitionSpec as P

MESH = pl.DeviceIdType.MESH
F32 = jnp.float32
BF16 = jnp.bfloat16
NB = 32
KB = 14
S = 32
G = 16
CAP = 4
COARSE = 512
CHUNKS = 7


def iota(shape, axis):
    return lax.broadcasted_iota(jnp.int32, shape, axis)


def hot(condition):
    return jnp.where(condition, 1.0, 0.0).astype(BF16)


def dot(a, b):
    return jnp.dot(a, b, preferred_element_type=F32)


def dot_t(a, b):
    return lax.dot_general(a, b, (((1,), (1,)), ((), ())), preferred_element_type=F32)


def lanes(v):
    return pl.ds(128 * v, 128)


def sub_peer(s, step):
    x = lax.rem(lax.div(s, 8) + lax.div(step, 8), 4)
    y = lax.rem(lax.div(s, 2) + lax.div(step, 2), 4)
    core = lax.rem(s + step, 2)
    return x * 8 + y * 2 + core


def group_peer(g, step):
    return lax.rem(g + step, G)


def ring(distance, length):
    return min(distance, length - distance)


SUB_STEPS = sorted(range(1, S), key=lambda v: -(ring(v // 8, 4) + ring(v // 2 % 4, 4) + 0.5 * (v % 2)))
GROUP_STEPS = sorted(range(1, G), key=lambda v: -ring(v, G))


def spread(x):
    x3 = x.reshape(NB, 8, 128)
    r3 = pltpu.roll(x, 64, 1).reshape(NB, 8, 128)
    low = iota((NB, 8, 128), 2) < 64
    parts = [jnp.where(low, x3, 0.0), jnp.where(low, r3, 0.0), jnp.where(low, 0.0, r3), jnp.where(low, 0.0, x3)]
    return jnp.concatenate(parts, axis=1).astype(BF16)


def kernel(
    schur, cols_hbm, basis_hbm, owner_hbm, target_hbm, inverse_hbm, cmap_hbm,
    corrected, matrix,
    cols, basis, owner, target, inverse, cmap, raw, packed, vecs, natural, rows_f32, select_t, table, send, arrive, right, pair, back, returned,
    left_g, high_g, low_g, terms, piece, pieces, final, load_sem, sem,
):
    g, s = lax.axis_index("group"), lax.axis_index("sub")

    def each(count, function):
        def body(step, carry):
            function(step)
            return carry

        lax.fori_loop(1, count, body, 0)

    def to_sub(source_of, into, k):
        def one(step):
            d = sub_peer(s, step)
            pltpu.make_async_remote_copy(
                src_ref=source_of(d), dst_ref=into.at[s], send_sem=sem.at[2 * k], recv_sem=sem.at[2 * k + 1],
                device_id={"sub": d}, device_id_type=MESH,
            ).start()

        for step in SUB_STEPS:
            one(step)

    def to_group(source_of, into, k):
        def one(step):
            d = group_peer(g, step)
            pltpu.make_async_remote_copy(
                src_ref=source_of(d), dst_ref=into.at[g], send_sem=sem.at[2 * k], recv_sem=sem.at[2 * k + 1],
                device_id={"group": d}, device_id_type=MESH,
            ).start()

        for step in GROUP_STEPS:
            one(step)

    def settle(buffer, count, which):
        part = buffer.at[pl.ds(0, count)]
        pltpu.make_async_copy(part, part, sem.at[which]).wait()

    barrier = pltpu.get_barrier_semaphore()
    each(S, lambda step: pl.semaphore_signal(barrier, 1, device_id={"sub": sub_peer(s, step)}, device_id_type=MESH))
    each(G, lambda step: pl.semaphore_signal(barrier, 1, device_id={"group": group_peer(g, step)}, device_id_type=MESH))

    per = KB // CHUNKS

    def load(c):
        part = pl.ds(per * c, per)
        return pltpu.make_async_copy(schur.at[part], raw.at[part], load_sem.at[c])

    small = [(owner_hbm, owner), (target_hbm, target), (cmap_hbm, cmap), (basis_hbm, basis), (cols_hbm, cols)]
    small = [pltpu.make_async_copy(a, b, load_sem.at[CHUNKS + v]) for v, (a, b) in enumerate(small)]
    for copy in small:
        copy.start()
    for c in range(CHUNKS):
        load(c).start()
    load_inverse = pltpu.make_async_copy(inverse_hbm, inverse, load_sem.at[CHUNKS + 5])
    load_inverse.start()
    for copy in small:
        copy.wait()

    lane32 = iota((NB, 128), 1)
    row32 = iota((NB, 128), 0)
    eye32 = iota((NB, NB), 0) == iota((NB, NB), 1)
    own = jnp.sum(jnp.where(eye32, owner[...], 0), axis=1, keepdims=True) == lane32 // CAP
    below = hot(iota((NB, NB), 1) < iota((NB, NB), 0))
    seen = dot(below, hot(own)).astype(jnp.int32)
    taken = own & (seen == lane32 % CAP)
    target_col = jnp.sum(jnp.where(eye32, target[...].astype(F32), 0.0), axis=1, keepdims=True)
    slot_target = jnp.sum(jnp.where(taken, target_col + 1.0, 0.0), axis=0, keepdims=True)
    slot_col = jnp.sum(jnp.where(taken, lane32.astype(F32), 0.0), axis=1, keepdims=True)
    slot_row = jnp.sum(jnp.where(eye32, slot_col, 0.0), axis=0, keepdims=True)
    eye16 = iota((16, 16), 0) == iota((16, 16), 1)
    cmap_col = jnp.sum(jnp.where(eye16, cmap[...], 0), axis=1, keepdims=True)
    lane16 = iota((16, 128), 1)
    ordered = (lane16 < 16) & (iota((16, 128), 0) == 2 * (lane16 % 8) + lane16 // 8)
    map_high = jnp.sum(jnp.where(ordered, (cmap_col // 16).astype(F32), 0.0), axis=0, keepdims=True)
    map_low = jnp.sum(jnp.where(ordered, (cmap_col % 16).astype(F32), 0.0), axis=0, keepdims=True)
    table[s] = jnp.concatenate([slot_target, map_high, map_low, jnp.zeros((5, 128), F32)], axis=0)

    flat = jnp.concatenate([basis[:, lanes(u)] for u in range(8)], axis=0)
    r256, c256 = iota((256, 256), 0), iota((256, 256), 1)
    by_block = hot((c256 % NB == r256 // 8) & (c256 // NB == r256 % 8))
    nat = dot(by_block, flat)
    natural[...] = nat
    vecs[...] = spread(nat)

    regroup = hot((c256 % 16 == r256 // 16) & (c256 // 16 == r256 % 16))

    def unpack(k, half):
        at = pl.ds(16 * half, 16)
        sides = []
        for h in range(2):
            sides.append(jnp.concatenate([raw[k, at, lanes(16 * h + t)] for t in range(16)], axis=0))
        out = dot(regroup, jnp.concatenate(sides, axis=1)).astype(BF16)
        for h in range(2):
            for b in range(16):
                packed[16 * half + b, pl.ds(16 * h, 16), lanes(k)] = out[16 * b : 16 * b + 16, 128 * h : 128 * h + 128]

    for c in range(CHUNKS):
        load(c).wait()
        for k in range(per * c, per * c + per):
            for half in range(2):
                unpack(k, half)

    pl.semaphore_wait(barrier, S - 1 + G - 1)
    to_sub(lambda d: table.at[s], table, 0)

    def product(b):
        vectors = jnp.concatenate([vecs[cols[k, 0, b]] for k in range(KB)], axis=1)
        out = jnp.concatenate([dot_t(vectors, packed[b])] * 4, axis=1)
        return [out[8 * v : 8 * v + 8] for v in range(4)]

    group8 = iota((8, 128), 1) // 32

    def first(b, carry):
        r = product(b)
        value = jnp.where(group8 == 0, r[0], jnp.where(group8 == 1, r[1], jnp.where(group8 == 2, r[2], r[3])))
        rows_f32[pl.ds(pl.multiple_of(8 * b, 8), 8), :] = value
        return carry

    lax.fori_loop(0, NB, first, 0, unroll=8)

    widen = hot(iota((NB, 256), 1) // 8 == iota((NB, 256), 0))
    slot_lane = dot(jnp.broadcast_to(slot_row, (8, NB)).astype(BF16), widen)[0:1].astype(jnp.int32)
    code = slot_lane // CAP * 32 + iota((1, 256), 1) % 8 * CAP + slot_lane % CAP
    select = hot(iota((1024, 256), 0) == code)
    send[...] = dot(select, rows_f32[...].astype(BF16)).astype(BF16).reshape(S, 32, 128)
    to_sub(lambda d: send.at[d], arrive, 1)
    arrive[s] = send[s]

    tall = hot(iota((256, NB), 0) // 8 == iota((256, NB), 1))
    slot_tall = dot(tall, jnp.broadcast_to(slot_col, (NB, 128)).astype(BF16)).astype(jnp.int32)
    code_tall = slot_tall // CAP * 32 + iota((256, 128), 0) % 8 * CAP + slot_tall % CAP
    for v in range(8):
        select_t[:, lanes(v)] = hot(iota((256, 128), 1) + 128 * v == code_tall)

    load_inverse.wait()
    for jg in range(4):
        tiles = jnp.stack([inverse[pl.ds(8 * jg, 8), lanes(t)] for t in range(32)], axis=0)
        block = jnp.swapaxes(tiles, 0, 1)
        turned = pltpu.roll(block.reshape(256, 128), 64, 1).reshape(8, 32, 128)
        low = iota((8, 32, 128), 2) < 64
        parts = [jnp.where(low, block, 0.0), jnp.where(low, 0.0, turned), jnp.where(low, turned, 0.0), jnp.where(low, 0.0, block)]
        full = jnp.concatenate(parts, axis=1)
        top = full.astype(BF16)
        right[pl.ds(8 * jg, 8), pl.ds(0, 128)] = top
        right[pl.ds(8 * jg, 8), pl.ds(128, 128)] = (full - top.astype(F32)).astype(BF16)

    settle(table, S - 1, 1)
    mine = jnp.where(lane32 // CAP == s, table[:, 0, :], 0.0).astype(BF16)
    by_slot = hot(iota((128, 1024), 0) % CAP == iota((128, 1024), 1) % CAP)
    spread_slot = dot(mine, by_slot)
    named = jnp.sum(jnp.where(iota((NB, 1024), 0) == iota((NB, 1024), 1) // 32, spread_slot, 0.0), axis=0, keepdims=True)
    code_in = (named.astype(jnp.int32) - 1) * 8 + iota((1, 1024), 1) // CAP % 8
    gather = hot(iota((256, 1024), 0) == code_in)
    by_source = hot(iota((1024, NB), 0) // 32 == iota((1024, NB), 1))
    tall_slot = dot(by_source, mine)
    kept = jnp.where(iota((1024, 128), 0) % CAP == iota((1024, 128), 1) % CAP, tall_slot, 0.0).astype(BF16)
    named_t = dot(kept, jnp.full((128, 256), 1.0, BF16)).astype(jnp.int32)
    gather_t = hot(iota((1024, 256), 1) == (named_t - 1) * 8 + iota((1024, 256), 0) // CAP % 8)

    settle(arrive, S - 1, 3)
    assembled = dot(gather, arrive[...].reshape(1024, 128))
    high = assembled.astype(BF16).astype(F32)
    pair[...] = jnp.concatenate(
        [high.reshape(NB, 8, 128), (assembled - high).reshape(NB, 8, 128)], axis=1
    ).astype(BF16)

    def correct(j, carry):
        out = dot(jnp.concatenate([pair[j], pair[j]], axis=1), right[j])
        rows_f32[pl.ds(pl.multiple_of(8 * j, 8), 8), :] = out[0:8] + out[8:16]
        return carry

    lax.fori_loop(0, NB, correct, 0, unroll=8)
    back[...] = dot(gather_t, rows_f32[...].astype(BF16)).astype(BF16).reshape(S, 32, 128)
    to_sub(lambda d: back.at[d], returned, 2)
    returned[s] = back[s]
    for u in range(8):
        corrected[:, lanes(u)] = rows_f32[pl.ds(u, NB, stride=8), :]

    erep_l = iota((128, 256), 1)
    copies = hot(iota((128, 256), 0) == erep_l // 128 * 16 + erep_l % 16)
    maps_h = table[:, 1, :].astype(BF16)
    maps_l = table[:, 2, :].astype(BF16)
    ll = iota((128, 1024), 1)
    pick = hot(iota((128, 1024), 0) == ll // 64 % 2 * 8 + ll % 8)
    source = ll[0:NB] // 256 * 8 + ll[0:NB] // 8 % 8
    is_source = iota((NB, 1024), 0) == source
    lane_h = jnp.sum(jnp.where(is_source, dot(maps_h, pick), 0.0), axis=0, keepdims=True).astype(jnp.int32)
    lane_l = jnp.sum(jnp.where(is_source, dot(maps_l, pick), 0.0), axis=0, keepdims=True).astype(jnp.int32)
    rows_mine = hot((iota((16, 1024), 0) == lane_l) & (lane_h == s))
    tall_s = hot(iota((512, NB), 0) // 16 == iota((512, NB), 1))
    own_lane = iota((512, 128), 0) % 16 == iota((512, 128), 1)
    col_h = jnp.where(own_lane, dot(tall_s, maps_h), 0.0).astype(BF16)
    col_l = jnp.where(own_lane, dot(tall_s, maps_l), 0.0).astype(BF16)
    ones = jnp.full((128, COARSE), 1.0, BF16)
    place = (dot(col_h, ones) * 16.0 + dot(col_l, ones)).astype(jnp.int32)
    spread_cols = hot(place == iota((512, COARSE), 1))

    settle(returned, S - 1, 5)
    from_owner = dot(select_t[...], returned[...].reshape(1024, 128))
    adjusted = (natural[...] - from_owner).astype(BF16)
    vecs[...] = spread(adjusted.astype(F32))
    q_row, q_col = iota((128, 128), 0), iota((128, 128), 1)
    reorder = hot((q_row // 64 == q_col // 32 % 2) & (q_row % 2 == q_col // 64) & (q_row % 64 // 2 == q_col % 32))
    message = dot(adjusted, reorder).reshape(NB, 8, 128)
    for b in range(NB):
        left_g[:, lanes(b)] = jnp.concatenate([message[b], jnp.zeros((8, 128), F32)], axis=0).astype(BF16)

    def second(b, carry):
        r = product(b)
        at_low = group8 < 2
        p_low = group8 % 2 == 0
        one, two = jnp.where(at_low, r[0], r[2]), jnp.where(at_low, r[1], r[3])
        rows = jnp.concatenate(
            [jnp.where(p_low, one, 0.0), jnp.where(p_low, two, 0.0), jnp.where(p_low, 0.0, one), jnp.where(p_low, 0.0, two)],
            axis=0,
        )
        top = rows.astype(BF16)
        at = pl.ds(pl.multiple_of(128 * b, 128), 128)
        high_g[:, at] = top
        low_g[:, at] = (rows - top.astype(F32)).astype(BF16)
        return carry

    lax.fori_loop(0, NB, second, 0, unroll=8)
    galerkin = (dot_t(left_g[...], high_g[...]) + dot_t(left_g[...], low_g[...])) * (NB * 64) ** -0.5
    terms[s] = jnp.concatenate([galerkin[0:8], jnp.zeros((8, 96), F32)], axis=1)
    to_sub(lambda d: terms.at[s], terms, 3)

    settle(terms, S - 1, 7)
    every = terms[...].reshape(256, 128)
    top = every.astype(BF16)
    both = jnp.concatenate([top, (every - top.astype(F32)).astype(BF16)], axis=0)
    wide = dot(both, copies)
    wide_row, wide_lane = iota((512, 256), 0), iota((512, 256), 1)
    wide = jnp.where(wide_row // 8 % 8 == wide_lane // 16 % 8, wide, 0.0).astype(BF16)
    parts = []
    for v in range(4):
        pieces_v = [wide[256 * h + 64 * v : 256 * h + 64 * v + 64, 128 * p : 128 * p + 128] for h in range(2) for p in range(2)]
        parts.append(dot(rows_mine[:, 256 * v : 256 * v + 256], jnp.concatenate(pieces_v, axis=0)))
    part = jnp.concatenate(parts, axis=1)
    p1 = part.astype(BF16).astype(F32)
    p2 = (part - p1).astype(BF16).astype(F32)
    p3 = part - p1 - p2
    out = dot(jnp.concatenate([p1, p2, p3], axis=0).astype(BF16), spread_cols)
    out = out[0:16] + out[16:32] + out[32:48]
    for v in range(G):
        piece[v] = out[4 * (v // 4) : 4 * (v // 4) + 4, 128 * (v % 4) : 128 * (v % 4) + 128]
    to_group(lambda d: piece.at[d], pieces, 4)
    pieces[g] = piece[g]
    settle(pieces, G - 1, 9)
    total = pieces[0]
    for v in range(1, G):
        total = total + pieces[v]
    final[g] = total
    to_group(lambda d: final.at[g], final, 5)
    settle(final, G - 1, 11)
    for v in range(G):
        matrix[pl.ds(4 * (v // 4), 4), lanes(v % 4)] = final[v]

    settle(table, S - 1, 0)
    settle(send, S - 1, 2)
    settle(back, S - 1, 4)
    settle(terms, S - 1, 6)
    settle(piece, G - 1, 8)
    settle(final, G - 1, 10)


def on_device(schur_blocks, block_cols, basis, owners, targets, inverses, coarse_map):
    vmem = pl.BlockSpec(memory_space=pltpu.VMEM)
    corrected, matrix = pl.pallas_call(
        kernel,
        out_shape=(jax.ShapeDtypeStruct((NB, 1024), F32), jax.ShapeDtypeStruct((16, COARSE), F32)),
        in_specs=[pl.BlockSpec(memory_space=pltpu.HBM)] * 7,
        out_specs=(vmem, vmem),
        scratch_shapes=[
            pltpu.SMEM((KB, 1, NB), jnp.int32),
            pltpu.VMEM((NB, 1024), BF16),
            pltpu.VMEM((1, NB), jnp.int32),
            pltpu.VMEM((1, NB), jnp.int32),
            pltpu.VMEM((NB, 4096), F32),
            pltpu.VMEM((1, 16), jnp.int32),
            pltpu.VMEM((KB, NB, 4096), BF16),
            pltpu.VMEM((NB, 32, 128 * KB), BF16),
            pltpu.VMEM((NB, 32, 128), BF16),
            pltpu.VMEM((256, 128), F32),
            pltpu.VMEM((256, 128), F32),
            pltpu.VMEM((256, 1024), BF16),
            pltpu.VMEM((S, 8, 128), F32),
            pltpu.VMEM((S, 32, 128), BF16),
            pltpu.VMEM((S, 32, 128), BF16),
            pltpu.VMEM((NB, 256, 128), BF16),
            pltpu.VMEM((NB, 16, 128), BF16),
            pltpu.VMEM((S, 32, 128), BF16),
            pltpu.VMEM((S, 32, 128), BF16),
            pltpu.VMEM((16, 128 * NB), BF16),
            pltpu.VMEM((32, 128 * NB), BF16),
            pltpu.VMEM((32, 128 * NB), BF16),
            pltpu.VMEM((S, 8, 128), F32),
            pltpu.VMEM((G, 4, 128), F32),
            pltpu.VMEM((G, 4, 128), F32),
            pltpu.VMEM((G, 4, 128), F32),
            pltpu.SemaphoreType.DMA((CHUNKS + 6,)),
            pltpu.SemaphoreType.DMA((12,)),
        ],
        compiler_params=pltpu.CompilerParams(
            collective_id=0, has_side_effects=True, vmem_limit_bytes=62 * 1024 * 1024
        ),
        name="setup_pass",
    )(
        jnp.swapaxes(schur_blocks[0, 0], 0, 1),
        jnp.transpose(block_cols, (0, 3, 1, 2))[0],
        basis[0, 0],
        owners[0, :, :, 0],
        targets[0],
        inverses[0, 0],
        coarse_map[0],
    )
    return corrected[None, None], matrix


def solution(mesh):
    return jax.shard_map(
        on_device,
        mesh=mesh,
        in_specs=(
            P("group", "sub", None, None, None),
            P("group", "sub", None, None),
            P("group", "sub", None, None),
            P("group", "sub", None, None),
            P("group", "sub", None),
            P("group", "sub", None, None),
            P("group", "sub", None),
        ),
        out_specs=(P("group", "sub", None, None), P("sub", None)),
        check_vma=False,
    )
```

```python
import functools

import jax
import jax.numpy as jnp
from jax import lax
from jax.experimental import pallas as pl
from jax.experimental.pallas import tpu as pltpu
from jax.sharding import PartitionSpec as P

MESH = pl.DeviceIdType.MESH
F32 = jnp.float32
BF16 = jnp.bfloat16
NB = 32
KB = 14
S = 32
G = 16
CAP = 4
COARSE = 512
CHUNKS = 7


def iota(shape, axis):
    return lax.broadcasted_iota(jnp.int32, shape, axis)


def hot(condition):
    return jnp.where(condition, 1.0, 0.0).astype(BF16)


def dot(a, b):
    return jnp.dot(a, b, preferred_element_type=F32)


def dot_t(a, b):
    return lax.dot_general(a, b, (((1,), (1,)), ((), ())), preferred_element_type=F32)


def lanes(v):
    return pl.ds(128 * v, 128)


def sub_peer(s, step):
    x = lax.rem(lax.div(s, 8) + lax.div(step, 8), 4)
    y = lax.rem(lax.div(s, 2) + lax.div(step, 2), 4)
    core = lax.rem(s + step, 2)
    return x * 8 + y * 2 + core


def group_peer(g, step):
    return lax.rem(g + step, G)


def ring(distance, length):
    return min(distance, length - distance)


SUB_STEPS = sorted(range(1, S), key=lambda v: -(ring(v // 8, 4) + ring(v // 2 % 4, 4) + 0.5 * (v % 2)))
GROUP_STEPS = sorted(range(1, G), key=lambda v: -ring(v, G))


def spread(x):
    x3 = x.reshape(NB, 8, 128)
    r3 = pltpu.roll(x, 64, 1).reshape(NB, 8, 128)
    low = iota((NB, 8, 128), 2) < 64
    parts = [jnp.where(low, x3, 0.0), jnp.where(low, r3, 0.0), jnp.where(low, 0.0, r3), jnp.where(low, 0.0, x3)]
    return jnp.concatenate(parts, axis=1).astype(BF16)


def kernel(
    schur, cols_hbm, basis_hbm, owner_hbm, target_hbm, inverse_hbm, cmap_hbm,
    corrected, matrix,
    cols, basis, owner, target, inverse, cmap, raw, packed, vecs, natural, rows_f32, select_t, table, send, arrive, right, pair, back, returned,
    left_g, high_g, low_g, maps_z, maps_s, terms_z, terms_s, spread_t, load_sem, sem,
):
    g, s = lax.axis_index("group"), lax.axis_index("sub")

    def each(count, function):
        def body(step, carry):
            function(step)
            return carry

        lax.fori_loop(1, count, body, 0)

    def to_sub(source_of, into, k, landing=lambda step: 0):
        def one(step):
            d = sub_peer(s, step)
            pltpu.make_async_remote_copy(
                src_ref=source_of(d), dst_ref=into.at[s], send_sem=sem.at[2 * k], recv_sem=sem.at[2 * k + 1 + landing(step)],
                device_id={"sub": d}, device_id_type=MESH,
            ).start()

        for step in SUB_STEPS:
            one(step)

    def to_group(source_of, into, k):
        def one(step):
            d = group_peer(g, step)
            pltpu.make_async_remote_copy(
                src_ref=source_of(d), dst_ref=into.at[g], send_sem=sem.at[2 * k], recv_sem=sem.at[2 * k + 1],
                device_id={"group": d}, device_id_type=MESH,
            ).start()

        for step in GROUP_STEPS:
            one(step)

    def settle(buffer, count, which):
        part = buffer.at[pl.ds(0, count)]
        pltpu.make_async_copy(part, part, sem.at[which]).wait()

    per = KB // CHUNKS

    def load(c):
        part = pl.ds(per * c, per)
        return pltpu.make_async_copy(schur.at[part], raw.at[part], load_sem.at[c])

    small = [(owner_hbm, owner), (target_hbm, target), (cmap_hbm, cmap), (basis_hbm, basis), (cols_hbm, cols)]
    small = [pltpu.make_async_copy(a, b, load_sem.at[CHUNKS + v]) for v, (a, b) in enumerate(small)]
    for copy in small:
        copy.start()
    for c in range(CHUNKS):
        load(c).start()
    load_inverse = pltpu.make_async_copy(inverse_hbm, inverse, load_sem.at[CHUNKS + 5])
    load_inverse.start()

    barrier = pltpu.get_barrier_semaphore()
    each(S, lambda step: pl.semaphore_signal(barrier, 1, device_id={"sub": sub_peer(s, step)}, device_id_type=MESH))
    each(G, lambda step: pl.semaphore_signal(barrier, 1, device_id={"group": group_peer(g, step)}, device_id_type=MESH))
    for copy in small:
        copy.wait()

    lane32 = iota((NB, 128), 1)
    row32 = iota((NB, 128), 0)
    eye32 = iota((NB, NB), 0) == iota((NB, NB), 1)
    own = jnp.sum(jnp.where(eye32, owner[...], 0), axis=1, keepdims=True) == lane32 // CAP
    below = hot(iota((NB, NB), 1) < iota((NB, NB), 0))
    seen = dot(below, hot(own)).astype(jnp.int32)
    taken = own & (seen == lane32 % CAP)
    target_col = jnp.sum(jnp.where(eye32, target[...].astype(F32), 0.0), axis=1, keepdims=True)
    slot_target = jnp.sum(jnp.where(taken, target_col + 1.0, 0.0), axis=0, keepdims=True)
    slot_col = jnp.sum(jnp.where(taken, lane32.astype(F32), 0.0), axis=1, keepdims=True)
    slot_row = jnp.sum(jnp.where(eye32, slot_col, 0.0), axis=0, keepdims=True)
    table[s] = jnp.concatenate([slot_target, jnp.zeros((7, 128), F32)], axis=0)
    row16, lane16 = iota((16, 16), 0), iota((16, 16), 1)
    cmap_col = jnp.sum(jnp.where(lane16 == 2 * (row16 % 8) + row16 // 8, cmap[...], 0), axis=1, keepdims=True)
    place16 = iota((16, 128), 1) // 16 == lax.rem(g, 8)
    maps_z[g] = jnp.where(place16, (cmap_col - COARSE // 2).astype(F32), 0.0).astype(BF16)

    flat = jnp.concatenate([basis[:, lanes(u)] for u in range(8)], axis=0)
    r256, c256 = iota((256, 256), 0), iota((256, 256), 1)
    by_block = hot((c256 % NB == r256 // 8) & (c256 // NB == r256 % 8))
    nat = dot(by_block, flat)
    natural[...] = nat
    vecs[...] = spread(nat)

    regroup = hot((c256 % 16 == r256 // 16) & (c256 // 16 == r256 % 16))

    def unpack(k, half):
        at = pl.ds(16 * half, 16)
        sides = []
        for h in range(2):
            sides.append(jnp.concatenate([raw[k, at, lanes(16 * h + t)] for t in range(16)], axis=0))
        out = dot(regroup, jnp.concatenate(sides, axis=1)).astype(BF16)
        for h in range(2):
            for b in range(16):
                packed[16 * half + b, pl.ds(16 * h, 16), lanes(k)] = out[16 * b : 16 * b + 16, 128 * h : 128 * h + 128]

    for c in range(CHUNKS):
        load(c).wait()
        for k in range(per * c, per * c + per):
            for half in range(2):
                unpack(k, half)

    pl.semaphore_wait(barrier, S - 1 + G - 1)
    to_sub(lambda d: table.at[s], table, 0)
    to_group(lambda d: maps_z.at[g], maps_z, 3)

    def product(b):
        vectors = jnp.concatenate([vecs[cols[k, 0, b]] for k in range(KB)], axis=1)
        out = jnp.concatenate([dot_t(vectors, packed[b])] * 4, axis=1)
        return [out[8 * v : 8 * v + 8] for v in range(4)]

    group8 = iota((8, 128), 1) // 32

    def first(b, carry):
        r = product(b)
        value = jnp.where(group8 == 0, r[0], jnp.where(group8 == 1, r[1], jnp.where(group8 == 2, r[2], r[3])))
        rows_f32[pl.ds(pl.multiple_of(8 * b, 8), 8), :] = value
        return carry

    lax.fori_loop(0, NB, first, 0, unroll=8)

    widen = hot(iota((NB, 256), 1) // 8 == iota((NB, 256), 0))
    slot_lane = dot(jnp.broadcast_to(slot_row, (8, NB)).astype(BF16), widen)[0:1].astype(jnp.int32)
    code = slot_lane // CAP * 32 + iota((1, 256), 1) % 8 * CAP + slot_lane % CAP
    select = hot(iota((1024, 256), 0) == code)
    send[...] = dot(select, rows_f32[...].astype(BF16)).astype(BF16).reshape(S, 32, 128)
    to_sub(lambda d: send.at[d], arrive, 1)
    arrive[s] = send[s]

    tall = hot(iota((256, NB), 0) // 8 == iota((256, NB), 1))
    slot_tall = dot(tall, jnp.broadcast_to(slot_col, (NB, 128)).astype(BF16)).astype(jnp.int32)
    code_tall = slot_tall // CAP * 32 + iota((256, 128), 0) % 8 * CAP + slot_tall % CAP
    for v in range(8):
        select_t[:, lanes(v)] = hot(iota((256, 128), 1) + 128 * v == code_tall)

    load_inverse.wait()
    for jg in range(4):
        tiles = jnp.stack([inverse[pl.ds(8 * jg, 8), lanes(t)] for t in range(32)], axis=0)
        block = jnp.swapaxes(tiles, 0, 1)
        turned = pltpu.roll(block.reshape(256, 128), 64, 1).reshape(8, 32, 128)
        low = iota((8, 32, 128), 2) < 64
        parts = [jnp.where(low, block, 0.0), jnp.where(low, 0.0, turned), jnp.where(low, turned, 0.0), jnp.where(low, 0.0, block)]
        full = jnp.concatenate(parts, axis=1)
        top = full.astype(BF16)
        right[pl.ds(8 * jg, 8), pl.ds(0, 128)] = top
        right[pl.ds(8 * jg, 8), pl.ds(128, 128)] = (full - top.astype(F32)).astype(BF16)

    settle(table, S - 1, 1)
    mine = jnp.where(lane32 // CAP == s, table[:, 0, :], 0.0).astype(BF16)
    by_slot = hot(iota((128, 1024), 0) % CAP == iota((128, 1024), 1) % CAP)
    spread_slot = dot(mine, by_slot)
    named = jnp.sum(jnp.where(iota((NB, 1024), 0) == iota((NB, 1024), 1) // 32, spread_slot, 0.0), axis=0, keepdims=True)
    code_in = (named.astype(jnp.int32) - 1) * 8 + iota((1, 1024), 1) // CAP % 8
    gather = hot(iota((256, 1024), 0) == code_in)
    by_source = hot(iota((1024, NB), 0) // 32 == iota((1024, NB), 1))
    tall_slot = dot(by_source, mine)
    kept = jnp.where(iota((1024, 128), 0) % CAP == iota((1024, 128), 1) % CAP, tall_slot, 0.0).astype(BF16)
    named_t = dot(kept, jnp.full((128, 256), 1.0, BF16)).astype(jnp.int32)
    gather_t = hot(iota((1024, 256), 1) == (named_t - 1) * 8 + iota((1024, 256), 0) // CAP % 8)

    settle(arrive, S - 1, 3)
    assembled = dot(gather, arrive[...].reshape(1024, 128))
    high = assembled.astype(BF16).astype(F32)
    pair[...] = jnp.concatenate(
        [high.reshape(NB, 8, 128), (assembled - high).reshape(NB, 8, 128)], axis=1
    ).astype(BF16)

    def correct(j, carry):
        out = dot(jnp.concatenate([pair[j], pair[j]], axis=1), right[j])
        rows_f32[pl.ds(pl.multiple_of(8 * j, 8), 8), :] = out[0:8] + out[8:16]
        return carry

    lax.fori_loop(0, NB, correct, 0, unroll=8)
    back[...] = dot(gather_t, rows_f32[...].astype(BF16)).astype(BF16).reshape(S, 32, 128)
    to_sub(lambda d: back.at[d], returned, 2)
    returned[s] = back[s]
    for u in range(8):
        corrected[:, lanes(u)] = rows_f32[pl.ds(u, NB, stride=8), :]

    def merge(parts, into):
        for h in range(2):
            total = parts[8 * h].astype(F32)
            for v in range(1, 8):
                total = total + parts[8 * h + v].astype(F32)
            into[s, :, lanes(h)] = total.astype(BF16)

    settle(maps_z, G - 1, 7)
    merge(maps_z, maps_s)
    to_sub(lambda d: maps_s.at[s], maps_s, 4)

    settle(returned, S - 1, 5)
    from_owner = dot(select_t[...], returned[...].reshape(1024, 128))
    adjusted = (natural[...] - from_owner).astype(BF16)
    vecs[...] = spread(adjusted.astype(F32))
    q_row, q_col = iota((128, 128), 0), iota((128, 128), 1)
    reorder = hot((q_row // 64 == q_col // 32 % 2) & (q_row % 2 == q_col // 64) & (q_row % 64 // 2 == q_col % 32))
    p_low = group8 % 2 == 0
    message = dot(adjusted, reorder).reshape(NB, 8, 128)
    for b in range(NB):
        left_g[:, lanes(b)] = jnp.concatenate(
            [jnp.where(p_low, message[b], 0.0), jnp.where(p_low, 0.0, message[b])], axis=0
        ).astype(BF16)

    def second(b, carry):
        r = product(b)
        at_low = group8 < 2
        rows = jnp.concatenate([jnp.where(at_low, r[0], r[2]), jnp.where(at_low, r[1], r[3])], axis=0)
        top = rows.astype(BF16)
        at = pl.ds(pl.multiple_of(128 * b, 128), 128)
        high_g[:, at] = top
        low_g[:, at] = (rows - top.astype(F32)).astype(BF16)
        return carry

    lax.fori_loop(0, NB, second, 0, unroll=8)
    galerkin = (dot_t(left_g[...], high_g[...]) + dot_t(left_g[...], low_g[...])) * (NB * 64) ** -0.5
    terms_z[g] = jnp.where(place16, jnp.concatenate([galerkin] * 8, axis=1), 0.0).astype(BF16)
    to_group(lambda d: terms_z.at[g], terms_z, 5)

    settle(maps_s, S - 1, 9)

    def columns(v, carry):
        maps = maps_s[v].astype(F32)
        diagonal = iota((16, 256), 0) == iota((16, 256), 1) % 16
        key = jnp.sum(jnp.where(diagonal, maps, 0.0), axis=0, keepdims=True).astype(jnp.int32) + COARSE // 2
        spread_t[:, pl.ds(pl.multiple_of(256 * v, 256), 256)] = hot(iota((COARSE, 256), 0) == key)
        return carry

    lax.fori_loop(0, S, columns, 0)
    settle(terms_z, G - 1, 11)
    merge(terms_z, terms_s)
    to_sub(lambda d: terms_s.at[s], terms_s, 6, lambda step: step // 8)

    row = iota((16, 256), 0).astype(F32) + (lax.convert_element_type(16 * s, F32) - COARSE // 2)

    def gather_rows(v):
        maps, values = maps_s[v].astype(F32), terms_s[v].astype(F32)
        total = jnp.zeros((16, 256), F32)
        for c in range(16):
            total = total + jnp.where(maps[c : c + 1] == row, values[c : c + 1], 0.0)
        top = total.astype(BF16)
        return jnp.concatenate([top, (total - top.astype(F32)).astype(BF16)], axis=0)

    def add(v, total):
        picked = jnp.concatenate([gather_rows(4 * v + w) for w in range(4)], axis=1)
        return total + dot_t(picked, spread_t[:, pl.ds(pl.multiple_of(1024 * v, 1024), 1024)])

    total = jnp.zeros((32, COARSE), F32)
    for dx in (0, 1, 3, 2):
        settle(terms_s, 8 if dx else 7, 13 + dx)
        first_of = 2 * lax.rem(lax.div(s, 8) + 4 - dx, 4)
        total = add(first_of + 1, add(first_of, total))
    matrix[...] = total[0:16] + total[16:32]

    settle(table, S - 1, 0)
    settle(send, S - 1, 2)
    settle(back, S - 1, 4)
    settle(maps_z, G - 1, 6)
    settle(maps_s, S - 1, 8)
    settle(terms_z, G - 1, 10)
    settle(terms_s, S - 1, 12)


def on_device(schur_blocks, block_cols, basis, owners, targets, inverses, coarse_map):
    hbm = pl.BlockSpec(memory_space=pltpu.HBM)
    shapes = (jax.ShapeDtypeStruct((NB, 1024), F32), jax.ShapeDtypeStruct((16, COARSE), F32))
    corrected, matrix = pl.pallas_call(
        kernel,
        out_shape=shapes,
        in_specs=[hbm] * 7,
        out_specs=(pl.BlockSpec(memory_space=pltpu.VMEM),) * 2,
        scratch_shapes=[
            pltpu.SMEM((KB, 1, NB), jnp.int32),
            pltpu.VMEM((NB, 1024), BF16),
            pltpu.VMEM((1, NB), jnp.int32),
            pltpu.VMEM((1, NB), jnp.int32),
            pltpu.VMEM((NB, 4096), F32),
            pltpu.VMEM((1, 16), jnp.int32),
            pltpu.VMEM((KB, NB, 4096), BF16),
            pltpu.VMEM((NB, 32, 128 * KB), BF16),
            pltpu.VMEM((NB, 32, 128), BF16),
            pltpu.VMEM((256, 128), F32),
            pltpu.VMEM((256, 128), F32),
            pltpu.VMEM((256, 1024), BF16),
            pltpu.VMEM((S, 8, 128), F32),
            pltpu.VMEM((S, 32, 128), BF16),
            pltpu.VMEM((S, 32, 128), BF16),
            pltpu.VMEM((NB, 256, 128), BF16),
            pltpu.VMEM((NB, 16, 128), BF16),
            pltpu.VMEM((S, 32, 128), BF16),
            pltpu.VMEM((S, 32, 128), BF16),
            pltpu.VMEM((16, 128 * NB), BF16),
            pltpu.VMEM((16, 128 * NB), BF16),
            pltpu.VMEM((16, 128 * NB), BF16),
            pltpu.VMEM((G, 16, 128), BF16),
            pltpu.VMEM((S, 16, 256), BF16),
            pltpu.VMEM((G, 16, 128), BF16),
            pltpu.VMEM((S, 16, 256), BF16),
            pltpu.VMEM((COARSE, 256 * S), BF16),
            pltpu.SemaphoreType.DMA((CHUNKS + 6,)),
            pltpu.SemaphoreType.DMA((17,)),
        ],
        compiler_params=pltpu.CompilerParams(
            collective_id=0, has_side_effects=True, vmem_limit_bytes=48 * 1024 * 1024
        ),
        name="setup_pass",
    )(
        *[
            pltpu.with_memory_space_constraint(x, pltpu.HBM)
            for x in (
                jnp.swapaxes(schur_blocks[0, 0], 0, 1),
                jnp.transpose(block_cols, (0, 3, 1, 2))[0],
                basis[0, 0],
                owners[0, :, :, 0],
                targets[0],
                inverses[0, 0],
                coarse_map[0],
            )
        ]
    )
    return corrected[None, None], matrix


def solution(mesh):
    return jax.shard_map(
        on_device,
        mesh=mesh,
        in_specs=(
            P("group", "sub", None, None, None),
            P("group", "sub", None, None),
            P("group", "sub", None, None),
            P("group", "sub", None, None),
            P("group", "sub", None),
            P("group", "sub", None, None),
            P("group", "sub", None),
        ),
        out_specs=(P("group", "sub", None, None), P("sub", None)),
        check_vma=False,
    )
```

```python
import functools

import jax
import jax.numpy as jnp
from jax import lax
from jax.experimental import pallas as pl
from jax.experimental.pallas import tpu as pltpu
from jax.sharding import PartitionSpec as P

MESH = pl.DeviceIdType.MESH
F32 = jnp.float32
BF16 = jnp.bfloat16
NB = 32
KB = 14
S = 32
G = 16
CAP = 4
COARSE = 512
CHUNKS = 7


def iota(shape, axis):
    return lax.broadcasted_iota(jnp.int32, shape, axis)


def hot(condition):
    return jnp.where(condition, 1.0, 0.0).astype(BF16)


def dot(a, b):
    return jnp.dot(a, b, preferred_element_type=F32)


def dot_t(a, b):
    return lax.dot_general(a, b, (((1,), (1,)), ((), ())), preferred_element_type=F32)


def lanes(v):
    return pl.ds(128 * v, 128)


def sub_peer(s, step):
    x = lax.rem(lax.div(s, 8) + lax.div(step, 8), 4)
    y = lax.rem(lax.div(s, 2) + lax.div(step, 2), 4)
    core = lax.rem(s + step, 2)
    return x * 8 + y * 2 + core


def group_peer(g, step):
    return lax.rem(g + step, G)


def ring(distance, length):
    return min(distance, length - distance)


SUB_STEPS = sorted(range(1, S), key=lambda v: -(ring(v // 8, 4) + ring(v // 2 % 4, 4) + 0.5 * (v % 2)))
GROUP_STEPS = sorted(range(1, G), key=lambda v: -ring(v, G))
NEAR = (1, 2, 3, 4, 13, 14, 15)


def spread(x):
    x3 = x.reshape(NB, 8, 128)
    r3 = pltpu.roll(x, 64, 1).reshape(NB, 8, 128)
    low = iota((NB, 8, 128), 2) < 64
    parts = [jnp.where(low, x3, 0.0), jnp.where(low, r3, 0.0), jnp.where(low, 0.0, r3), jnp.where(low, 0.0, x3)]
    return jnp.concatenate(parts, axis=1).astype(BF16)


def kernel(
    schur, cols_hbm, basis_hbm, owner_hbm, target_hbm, inverse_hbm, cmap_hbm,
    corrected, matrix,
    cols, basis, owner, target, inverse, cmap, raw, packed, vecs, natural, rows_f32, select_t, table, send, arrive, right, pair, back, returned,
    left_g, high_g, low_g, maps_z, maps_s, terms_z, terms_s, spread_t, load_sem, sem,
):
    g, s = lax.axis_index("group"), lax.axis_index("sub")

    def each(count, function):
        def body(step, carry):
            function(step)
            return carry

        lax.fori_loop(1, count, body, 0)

    def to_sub(source_of, into, sent, landed):
        for step in SUB_STEPS:
            d = sub_peer(s, step)
            pltpu.make_async_remote_copy(
                src_ref=source_of(d), dst_ref=into.at[s], send_sem=sem.at[sent], recv_sem=sem.at[landed(step)],
                device_id={"sub": d}, device_id_type=MESH,
            ).start()

    def to_group(source_of, into, sent, landed):
        for step in GROUP_STEPS:
            pltpu.make_async_remote_copy(
                src_ref=source_of(g), dst_ref=into.at[g], send_sem=sem.at[sent], recv_sem=sem.at[landed(step)],
                device_id={"group": group_peer(g, step)}, device_id_type=MESH,
            ).start()

    def settle(buffer, count, which):
        part = buffer.at[pl.ds(0, count)]
        pltpu.make_async_copy(part, part, sem.at[which]).wait()

    barrier = pltpu.get_barrier_semaphore()
    for step in GROUP_STEPS:
        pl.semaphore_signal(barrier, 1, device_id={"group": group_peer(g, step)}, device_id_type=MESH)
    per = KB // CHUNKS

    def load(c):
        part = pl.ds(per * c, per)
        return pltpu.make_async_copy(schur.at[part], raw.at[part], load_sem.at[c])

    small = [(owner_hbm, owner), (target_hbm, target), (cmap_hbm, cmap), (basis_hbm, basis), (cols_hbm, cols)]
    small = [pltpu.make_async_copy(a, b, load_sem.at[CHUNKS + v]) for v, (a, b) in enumerate(small)]
    for copy in small:
        copy.start()
    for c in range(CHUNKS):
        load(c).start()
    load_inverse = pltpu.make_async_copy(inverse_hbm, inverse, load_sem.at[CHUNKS + 5])
    each(S, lambda step: pl.semaphore_signal(barrier, 1, device_id={"sub": sub_peer(s, step)}, device_id_type=MESH))
    for copy in small:
        copy.wait()

    lane32 = iota((NB, 128), 1)
    row32 = iota((NB, 128), 0)
    eye32 = iota((NB, NB), 0) == iota((NB, NB), 1)
    own = jnp.sum(jnp.where(eye32, owner[...], 0), axis=1, keepdims=True) == lane32 // CAP
    below = hot(iota((NB, NB), 1) < iota((NB, NB), 0))
    seen = dot(below, hot(own)).astype(jnp.int32)
    taken = own & (seen == lane32 % CAP)
    target_col = jnp.sum(jnp.where(eye32, target[...].astype(F32), 0.0), axis=1, keepdims=True)
    slot_target = jnp.sum(jnp.where(taken, target_col + 1.0, 0.0), axis=0, keepdims=True)
    slot_col = jnp.sum(jnp.where(taken, lane32.astype(F32), 0.0), axis=1, keepdims=True)
    slot_row = jnp.sum(jnp.where(eye32, slot_col, 0.0), axis=0, keepdims=True)
    table[s] = jnp.concatenate([slot_target, jnp.zeros((7, 128), F32)], axis=0)
    row16, lane16 = iota((16, 16), 0), iota((16, 16), 1)
    cmap_col = jnp.sum(jnp.where(lane16 == 2 * (row16 % 8) + row16 // 8, cmap[...], 0), axis=1, keepdims=True)
    place16 = iota((16, 128), 1) // 16 == lax.rem(g, 8)
    maps_z[g] = jnp.where(place16, (cmap_col - COARSE // 2).astype(F32), 0.0).astype(BF16)

    flat = jnp.concatenate([basis[:, lanes(u)] for u in range(8)], axis=0)
    r256, c256 = iota((256, 256), 0), iota((256, 256), 1)
    by_block = hot((c256 % NB == r256 // 8) & (c256 // NB == r256 % 8))
    nat = dot(by_block, flat)
    natural[...] = nat
    vecs[...] = spread(nat)

    regroup = hot((c256 % 16 == r256 // 16) & (c256 // 16 == r256 % 16))

    def unpack(k, half):
        at = pl.ds(16 * half, 16)
        sides = []
        for h in range(2):
            sides.append(jnp.concatenate([raw[k, at, lanes(16 * h + t)] for t in range(16)], axis=0))
        out = dot(regroup, jnp.concatenate(sides, axis=1)).astype(BF16)
        for h in range(2):
            for b in range(16):
                packed[16 * half + b, pl.ds(16 * h, 16), lanes(k)] = out[16 * b : 16 * b + 16, 128 * h : 128 * h + 128]

    for c in range(CHUNKS):
        load(c).wait()
        for k in range(per * c, per * c + per):
            for half in range(2):
                unpack(k, half)

    load_inverse.start()

    def product(b):
        vectors = jnp.concatenate([vecs[cols[k, 0, b]] for k in range(KB)], axis=1)
        out = jnp.concatenate([dot_t(vectors, packed[b])] * 4, axis=1)
        return [out[8 * v : 8 * v + 8] for v in range(4)]

    group8 = iota((8, 128), 1) // 32

    def first(b, carry):
        r = product(b)
        value = jnp.where(group8 == 0, r[0], jnp.where(group8 == 1, r[1], jnp.where(group8 == 2, r[2], r[3])))
        rows_f32[pl.ds(pl.multiple_of(8 * b, 8), 8), :] = value
        return carry

    lax.fori_loop(0, NB, first, 0, unroll=8)

    widen = hot(iota((NB, 256), 1) // 8 == iota((NB, 256), 0))
    slot_lane = dot(jnp.broadcast_to(slot_row, (8, NB)).astype(BF16), widen)[0:1].astype(jnp.int32)
    code = slot_lane // CAP * 32 + iota((1, 256), 1) % 8 * CAP + slot_lane % CAP
    select = hot(iota((1024, 256), 0) == code)
    send[...] = dot(select, rows_f32[...].astype(BF16)).astype(BF16).reshape(S, 32, 128)
    pl.semaphore_wait(barrier, S - 1 + G - 1)
    to_sub(lambda d: table.at[s], table, 0, lambda step: 1)
    to_sub(lambda d: send.at[d], arrive, 2, lambda step: 3)
    to_group(lambda d: maps_z.at[d], maps_z, 6, lambda step: 7)
    arrive[s] = send[s]

    tall = hot(iota((256, NB), 0) // 8 == iota((256, NB), 1))
    slot_tall = dot(tall, jnp.broadcast_to(slot_col, (NB, 128)).astype(BF16)).astype(jnp.int32)
    code_tall = slot_tall // CAP * 32 + iota((256, 128), 0) % 8 * CAP + slot_tall % CAP
    for v in range(8):
        select_t[:, lanes(v)] = hot(iota((256, 128), 1) + 128 * v == code_tall)

    load_inverse.wait()
    for jg in range(4):
        tiles = jnp.stack([inverse[pl.ds(8 * jg, 8), lanes(t)] for t in range(32)], axis=0)
        block = jnp.swapaxes(tiles, 0, 1)
        turned = pltpu.roll(block.reshape(256, 128), 64, 1).reshape(8, 32, 128)
        low = iota((8, 32, 128), 2) < 64
        parts = [jnp.where(low, block, 0.0), jnp.where(low, 0.0, turned), jnp.where(low, turned, 0.0), jnp.where(low, 0.0, block)]
        full = jnp.concatenate(parts, axis=1)
        top = full.astype(BF16)
        right[pl.ds(8 * jg, 8), pl.ds(0, 128)] = top
        right[pl.ds(8 * jg, 8), pl.ds(128, 128)] = (full - top.astype(F32)).astype(BF16)

    settle(table, S - 1, 1)
    mine = jnp.where(lane32 // CAP == s, table[:, 0, :], 0.0).astype(BF16)
    by_slot = hot(iota((128, 1024), 0) % CAP == iota((128, 1024), 1) % CAP)
    spread_slot = dot(mine, by_slot)
    named = jnp.sum(jnp.where(iota((NB, 1024), 0) == iota((NB, 1024), 1) // 32, spread_slot, 0.0), axis=0, keepdims=True)
    code_in = (named.astype(jnp.int32) - 1) * 8 + iota((1, 1024), 1) // CAP % 8
    gather = hot(iota((256, 1024), 0) == code_in)
    by_source = hot(iota((1024, NB), 0) // 32 == iota((1024, NB), 1))
    tall_slot = dot(by_source, mine)
    kept = jnp.where(iota((1024, 128), 0) % CAP == iota((1024, 128), 1) % CAP, tall_slot, 0.0).astype(BF16)
    named_t = dot(kept, jnp.full((128, 256), 1.0, BF16)).astype(jnp.int32)
    gather_t = hot(iota((1024, 256), 1) == (named_t - 1) * 8 + iota((1024, 256), 0) // CAP % 8)

    settle(arrive, S - 1, 3)
    assembled = dot(gather, arrive[...].reshape(1024, 128))
    high = assembled.astype(BF16).astype(F32)
    pair[...] = jnp.concatenate(
        [high.reshape(NB, 8, 128), (assembled - high).reshape(NB, 8, 128)], axis=1
    ).astype(BF16)

    def correct(j, carry):
        out = dot(jnp.concatenate([pair[j], pair[j]], axis=1), right[j])
        rows_f32[pl.ds(pl.multiple_of(8 * j, 8), 8), :] = out[0:8] + out[8:16]
        return carry

    lax.fori_loop(0, NB, correct, 0, unroll=8)
    back[...] = dot(gather_t, rows_f32[...].astype(BF16)).astype(BF16).reshape(S, 32, 128)
    to_sub(lambda d: back.at[d], returned, 4, lambda step: 5)
    returned[s] = back[s]
    for u in range(8):
        corrected[:, lanes(u)] = rows_f32[pl.ds(u, NB, stride=8), :]

    def merged(parts, half):
        total = parts[lax.rem(g + (4 if half else 12), G)].astype(F32)
        for v in range(1, 8):
            total = total + parts[lax.rem(g + (4 if half else 12) + v, G)].astype(F32)
        return total.astype(BF16)

    settle(returned, S - 1, 5)
    from_owner = dot(select_t[...], returned[...].reshape(1024, 128))
    adjusted = (natural[...] - from_owner).astype(BF16)
    vecs[...] = spread(adjusted.astype(F32))
    q_row, q_col = iota((128, 128), 0), iota((128, 128), 1)
    reorder = hot((q_row // 64 == q_col // 32 % 2) & (q_row % 2 == q_col // 64) & (q_row % 64 // 2 == q_col % 32))
    p_low = group8 % 2 == 0
    message = dot(adjusted, reorder).reshape(NB, 8, 128)
    for b in range(NB):
        left_g[:, lanes(b)] = jnp.concatenate(
            [jnp.where(p_low, message[b], 0.0), jnp.where(p_low, 0.0, message[b])], axis=0
        ).astype(BF16)

    def second(b, carry):
        r = product(b)
        at_low = group8 < 2
        rows = jnp.concatenate([jnp.where(at_low, r[0], r[2]), jnp.where(at_low, r[1], r[3])], axis=0)
        top = rows.astype(BF16)
        at = pl.ds(pl.multiple_of(128 * b, 128), 128)
        high_g[:, at] = top
        low_g[:, at] = (rows - top.astype(F32)).astype(BF16)
        return carry

    lax.fori_loop(0, NB, second, 0, unroll=8)
    galerkin = (dot_t(left_g[...], high_g[...]) + dot_t(left_g[...], low_g[...])) * (NB * 64) ** -0.5
    terms_z[g] = jnp.where(place16, jnp.concatenate([galerkin] * 8, axis=1), 0.0).astype(BF16)
    to_group(lambda d: terms_z.at[d], terms_z, 10, lambda step: 11 if step in NEAR else 12)

    settle(maps_z, G - 1, 7)
    for half in range(2):
        maps_s[s, half] = merged(maps_z, half)
    to_sub(lambda d: maps_s.at[s], maps_s, 8, lambda step: 9)

    settle(terms_z, 7, 11)
    terms_s[0, s] = merged(terms_z, 0)
    to_sub(lambda d: terms_s.at[0, s], terms_s.at[0], 13, lambda step: 14)
    settle(terms_z, 8, 12)
    terms_s[1, s] = merged(terms_z, 1)
    to_sub(lambda d: terms_s.at[1, s], terms_s.at[1], 15, lambda step: 16 + step // 8)

    settle(maps_s, S - 1, 9)

    def columns(v, carry):
        diagonal = iota((16, 128), 0) == iota((16, 128), 1) % 16
        for half in range(2):
            maps = maps_s[v, half].astype(F32)
            key = jnp.sum(jnp.where(diagonal, maps, 0.0), axis=0, keepdims=True).astype(jnp.int32) + COARSE // 2
            spread_t[:, pl.ds(pl.multiple_of(4096 * half + 128 * v, 128), 128)] = hot(iota((COARSE, 128), 0) == key)
        return carry

    lax.fori_loop(0, S, columns, 0, unroll=2)

    row = iota((16, 128), 0).astype(F32) + (lax.convert_element_type(16 * s, F32) - COARSE // 2)

    def gather_rows(half, v):
        maps, values = maps_s[v, half].astype(F32), terms_s[half, v].astype(F32)
        total = jnp.zeros((16, 128), F32)
        for c in range(16):
            total = total + jnp.where(maps[c : c + 1] == row, values[c : c + 1], 0.0)
        top = total.astype(BF16)
        return jnp.concatenate([top, (total - top.astype(F32)).astype(BF16)], axis=0)

    def add(half, x, total):
        picked = jnp.concatenate([gather_rows(half, 8 * x + w) for w in range(8)], axis=1)
        at = 4096 * half + 1024 * x
        return total + dot_t(picked, spread_t[:, pl.ds(at if isinstance(at, int) else pl.multiple_of(at, 1024), 1024)])

    settle(terms_s.at[0], S - 1, 14)
    total = jnp.zeros((32, COARSE), F32)
    for x in range(4):
        total = add(0, x, total)
    for dx in (0, 1, 3, 2):
        settle(terms_s.at[1], 8 if dx else 7, 16 + dx)
        total = add(1, lax.rem(lax.div(s, 8) + 4 - dx, 4), total)
    matrix[...] = total[0:16] + total[16:32]

    settle(table, S - 1, 0)
    settle(send, S - 1, 2)
    settle(back, S - 1, 4)
    settle(maps_z, G - 1, 6)
    settle(maps_s, S - 1, 8)
    settle(terms_z, G - 1, 10)
    settle(terms_s.at[0], S - 1, 13)
    settle(terms_s.at[1], S - 1, 15)


def on_device(schur_blocks, block_cols, basis, owners, targets, inverses, coarse_map):
    hbm = pl.BlockSpec(memory_space=pltpu.HBM)
    shapes = (jax.ShapeDtypeStruct((NB, 1024), F32), jax.ShapeDtypeStruct((16, COARSE), F32))
    corrected, matrix = pl.pallas_call(
        kernel,
        out_shape=shapes,
        in_specs=[hbm] * 7,
        out_specs=(pl.BlockSpec(memory_space=pltpu.VMEM),) * 2,
        scratch_shapes=[
            pltpu.SMEM((KB, 1, NB), jnp.int32),
            pltpu.VMEM((NB, 1024), BF16),
            pltpu.VMEM((1, NB), jnp.int32),
            pltpu.VMEM((1, NB), jnp.int32),
            pltpu.VMEM((NB, 4096), F32),
            pltpu.VMEM((1, 16), jnp.int32),
            pltpu.VMEM((KB, NB, 4096), BF16),
            pltpu.VMEM((NB, 32, 128 * KB), BF16),
            pltpu.VMEM((NB, 32, 128), BF16),
            pltpu.VMEM((256, 128), F32),
            pltpu.VMEM((256, 128), F32),
            pltpu.VMEM((256, 1024), BF16),
            pltpu.VMEM((S, 8, 128), F32),
            pltpu.VMEM((S, 32, 128), BF16),
            pltpu.VMEM((S, 32, 128), BF16),
            pltpu.VMEM((NB, 256, 128), BF16),
            pltpu.VMEM((NB, 16, 128), BF16),
            pltpu.VMEM((S, 32, 128), BF16),
            pltpu.VMEM((S, 32, 128), BF16),
            pltpu.VMEM((16, 128 * NB), BF16),
            pltpu.VMEM((16, 128 * NB), BF16),
            pltpu.VMEM((16, 128 * NB), BF16),
            pltpu.VMEM((G, 16, 128), BF16),
            pltpu.VMEM((S, 2, 16, 128), BF16),
            pltpu.VMEM((G, 16, 128), BF16),
            pltpu.VMEM((2, S, 16, 128), BF16),
            pltpu.VMEM((COARSE, 256 * S), BF16),
            pltpu.SemaphoreType.DMA((CHUNKS + 6,)),
            pltpu.SemaphoreType.DMA((20,)),
        ],
        compiler_params=pltpu.CompilerParams(
            collective_id=0, has_side_effects=True, vmem_limit_bytes=48 * 1024 * 1024
        ),
        name="setup_pass",
    )(
        *[
            pltpu.with_memory_space_constraint(x, pltpu.HBM)
            for x in (
                jnp.swapaxes(schur_blocks[0, 0], 0, 1),
                jnp.transpose(block_cols, (0, 3, 1, 2))[0],
                basis[0, 0],
                owners[0, :, :, 0],
                targets[0],
                inverses[0, 0],
                coarse_map[0],
            )
        ]
    )
    return corrected[None, None], matrix


def solution(mesh):
    return jax.shard_map(
        on_device,
        mesh=mesh,
        in_specs=(
            P("group", "sub", None, None, None),
            P("group", "sub", None, None),
            P("group", "sub", None, None),
            P("group", "sub", None, None),
            P("group", "sub", None),
            P("group", "sub", None, None),
            P("group", "sub", None),
        ),
        out_specs=(P("group", "sub", None, None), P("sub", None)),
        check_vma=False,
    )
```
